32 devices in a mesh: dp: 8 (over z, core), mp: 4 (over y, x).
Axes of the slice: x: 2, y: 2, z: 4, core: 2. Of those that a mesh axis runs over, the one named last changes fastest.
Arguments:
- layer_in: bfloat16 [1024, 4608], P('dp', 'mp'), may hold values from -6 to 6
- up_grad: bfloat16 [1024, 36864], P('dp', 'mp'), may hold values from -12 to 12
- hidden: bfloat16 [1024, 36864], P('dp', 'mp'), may hold values from -6 to 6
- out_grad: bfloat16 [1024, 4608], P('dp', 'mp'), may hold values from -12 to 12
- err_up_left: bfloat16 [8, 4608, 32], P('dp', 'mp'), may hold values from -12 to 12
- err_up_right: bfloat16 [8, 36864, 32], P('dp', 'mp'), may hold values from -12 to 12
- err_down_left: bfloat16 [8, 36864, 32], P('dp', 'mp'), may hold values from -12 to 12
- err_down_right: bfloat16 [8, 4608, 32], P('dp', 'mp'), may hold values from -12 to 12
- q_up: float32 [36864, 32], P('mp'), may hold values from -6 to 6
- q_down: float32 [4608, 32], P('mp'), may hold values from -6 to 6
- momentum_up: bfloat16 [4608, 36864], P('dp', 'mp'), may hold values from -4 to 4
- momentum_down: bfloat16 [36864, 4608], P('mp', 'dp'), may hold values from -4 to 4
Outputs:
- q_up_next: float32 [36864, 32], P('mp')
- q_down_next: float32 [4608, 32], P('mp')
- new_momentum_up: bfloat16 [4608, 36864], P('dp', 'mp')
- new_momentum_down: bfloat16 [36864, 4608], P('mp', 'dp')
The draws below stay inside these ranges and needn't reach their ends.
All inputs are finite; a program needn't handle non-finite values.
Results may differ from the reference program's by a relative error of at most 0.001.
Values sent between devices are 32-bit elements; how exact they have to be, the bound alone decides.
A program may use at most 128 MiB of HBM per device.

```python
import jax
import jax.numpy as jnp
from jax import lax

D = 4608
FF = 36864
R = 32
TOK_DEV = 128
REPLICAS = 8
TOKENS = 1024


def shard_levels(key, dims, cuts, least, top_value):
    loudness, own = 1.0, jax.random.fold_in(key, 6)
    for dim, shards_of in cuts:
        steps = jnp.exp(jax.random.uniform(jax.random.fold_in(own, dim), (shards_of,), jnp.float32, least / len(cuts), top_value / len(cuts)))
        loudness = loudness * jnp.repeat(steps, dims[dim] // shards_of).reshape([-1 if axis == dim else 1 for axis in range(len(dims))])
    return loudness


def gaussian(key, dims, deviation, most, pieces=(), dtype=jnp.bfloat16):
    values = jax.random.normal(key, dims, jnp.float32) * deviation
    if len(pieces) > 0:
        values = shard_levels(key, dims, pieces, -0.22, 0.18) * values
    return jnp.clip(values, min=-most, max=most).astype(dtype)


def setup_inputs(seed: int = 0) -> dict:
    streams_of = jax.random.split(jax.random.key(seed), 13)
    layer_in = gaussian(streams_of[0], (TOKENS, D), 1.0, 6.0, ((0, 8), (1, 4)))
    up_grad = gaussian(streams_of[1], (TOKENS, FF), 2.0, 12.0, ((0, 8), (1, 4)))
    hidden = gaussian(streams_of[2], (TOKENS, FF), 1.0, 6.0, ((0, 8), (1, 4)))
    out_grad = gaussian(streams_of[3], (TOKENS, D), 2.0, 12.0, ((0, 8), (1, 4)))
    err_up_left = gaussian(streams_of[4], (REPLICAS, D, R), 2.0, 12.0, ((0, 8), (1, 4)))
    err_up_right = gaussian(streams_of[5], (REPLICAS, FF, R), 2.0, 12.0, ((0, 8), (1, 4)))
    err_down_left = gaussian(streams_of[6], (REPLICAS, FF, R), 2.0, 12.0, ((0, 8), (1, 4)))
    err_down_right = gaussian(streams_of[7], (REPLICAS, D, R), 2.0, 12.0, ((0, 8), (1, 4)))
    q_up = gaussian(streams_of[8], (FF, R), 1.0, 6.0, ((0, 4),), jnp.float32)
    q_down = gaussian(streams_of[9], (D, R), 1.0, 6.0, ((0, 4),), jnp.float32)
    momentum_up = gaussian(streams_of[10], (D, FF), 0.5, 4.0, ((0, 8), (1, 4)))
    momentum_down = gaussian(streams_of[11], (FF, D), 0.5, 4.0, ((0, 4), (1, 8)))
    return dict(layer_in=layer_in, up_grad=up_grad, hidden=hidden, out_grad=out_grad, err_up_left=err_up_left, err_up_right=err_up_right, err_down_left=err_down_left, err_down_right=err_down_right, q_up=q_up, q_down=q_down, momentum_up=momentum_up, momentum_down=momentum_down)


def times(left, right):
    return jnp.dot(left.astype(jnp.float32), right.astype(jnp.float32), precision=lax.Precision.HIGHEST, preferred_element_type=jnp.float32)

def orthonormal(factor):
    gram = times(factor.T, factor)
    lower = jnp.linalg.cholesky(gram)
    return jax.scipy.linalg.solve_triangular(lower, factor.T, lower=True).T

def reference(layer_in, up_grad, hidden, out_grad, err_up_left, err_up_right, err_down_left, err_down_right, q_up, q_down, momentum_up, momentum_down):

    def blocks(array):
        return array.reshape(REPLICAS, TOK_DEV, array.shape[-1])
    items = (blocks(layer_in), blocks(up_grad), blocks(hidden), blocks(out_grad), err_up_left, err_up_right, err_down_left, err_down_right)

    def p_step(carry, item):
        x_rows, u_rows, h_rows, o_rows, eul, eur, edl, edr = item
        total_up = carry[0] + times(x_rows.T, times(u_rows, q_up)) + times(eul, times(eur.T, q_up))
        total_down = carry[1] + times(h_rows.T, times(o_rows, q_down)) + times(edl, times(edr.T, q_down))
        return ((total_up, total_down), None)
    start = (jnp.zeros((D, R), jnp.float32), jnp.zeros((FF, R), jnp.float32))
    (p_up, p_down), _ = lax.scan(p_step, start, items)
    orth_up = orthonormal(p_up / REPLICAS)
    orth_down = orthonormal(p_down / REPLICAS)

    def q_step(carry, item):
        x_rows, u_rows, h_rows, o_rows, eul, eur, edl, edr = item
        total_up = carry[0] + times(u_rows.T, times(x_rows, orth_up)) + times(eur, times(eul.T, orth_up))
        total_down = carry[1] + times(o_rows.T, times(h_rows, orth_down)) + times(edr, times(edl.T, orth_down))
        return ((total_up, total_down), None)
    start = (jnp.zeros((FF, R), jnp.float32), jnp.zeros((D, R), jnp.float32))
    (q_up_sum, q_down_sum), _ = lax.scan(q_step, start, items)
    q_up_next = q_up_sum / REPLICAS
    q_down_next = q_down_sum / REPLICAS

    def momentum_rows(item, right):
        return (0.9 * item[0].astype(jnp.float32) + times(item[1], right.T)).astype(jnp.bfloat16)
    new_momentum_up = lax.map(lambda item: momentum_rows(item, q_up_next), (momentum_up.reshape(8, D // 8, FF), orth_up.reshape(8, D // 8, R))).reshape(D, FF)
    new_momentum_down = lax.map(lambda item: momentum_rows(item, q_down_next), (momentum_down.reshape(8, FF // 8, D), orth_down.reshape(8, FF // 8, R))).reshape(FF, D)
    return (q_up_next, q_down_next, new_momentum_up, new_momentum_down)
```

```python
import functools

import jax
import jax.numpy as jnp
from jax import lax
from jax.experimental import pallas as pl
from jax.experimental.pallas import tpu as pltpu
from jax.sharding import PartitionSpec as P

F32 = jnp.float32
BF16 = jnp.bfloat16
MESH = pl.DeviceIdType.MESH
LANES = 128
MAX_CHUNK = 1152


def whole_tiles(width):
    return -(-width // LANES) * LANES


def chunk_of(width):
    if width % LANES:
        return width
    size = MAX_CHUNK
    while width % size:
        size -= LANES
    return size


def split3(x):
    hi = x.astype(BF16)
    rest = x - hi.astype(F32)
    mid = rest.astype(BF16)
    lo = (rest - mid.astype(F32)).astype(BF16)
    return jnp.concatenate([hi, mid, lo], axis=0)


def fold3(x):
    rank = x.shape[0] // 3
    return x[:rank] + x[rank : 2 * rank] + x[2 * rank :]


def dot_nt(a, b):
    return lax.dot_general(a, b, (((1,), (1,)), ((), ())), preferred_element_type=F32)


def dot_nn(a, b):
    return jnp.dot(a, b, preferred_element_type=F32)


def dot_small(a, b):
    return jnp.dot(a, b, precision=lax.Precision.HIGHEST, preferred_element_type=F32)


def project(x_ref, start, rows_ref, err_ref, with_gram):
    width = rows_ref.shape[1]
    step = chunk_of(width)
    outs = rows_ref.shape[0] + err_ref.shape[0] + (3 * err_ref.shape[0] if with_gram else 0)

    def body(i, acc):
        at = 0 if step == width else pl.multiple_of(i * step, LANES)
        x = split3(x_ref[:, pl.ds(start + at, step)])
        parts = [rows_ref[:, pl.ds(at, step)], err_ref[:, pl.ds(at, step)]]
        if with_gram:
            parts.append(x)
        return acc + dot_nt(x, jnp.concatenate(parts, axis=0))

    zero = jnp.zeros((3 * err_ref.shape[0], outs), F32)
    return body(0, zero) if step == width else lax.fori_loop(0, width // step, body, zero)


def expand(left, rows_ref, err_ref, out_ref, start):
    width = rows_ref.shape[1]
    step = chunk_of(width)
    stacked = split3(left)

    def body(i, carry):
        at = 0 if step == width else pl.multiple_of(i * step, LANES)
        right = jnp.concatenate([rows_ref[:, pl.ds(at, step)], err_ref[:, pl.ds(at, step)]], axis=0)
        out_ref[:, pl.ds(start + at, step)] = fold3(dot_nn(stacked, right))
        return carry

    if step == width:
        body(0, 0)
    else:
        lax.fori_loop(0, width // step, body, 0)


def gram_and_projections(acc, tokens):
    rank = acc.shape[0] // 3
    high, middle = acc[:rank], acc[rank : 2 * rank]
    low = acc[2 * rank :]
    total = high + middle + low
    tail = total[:, tokens:]
    both = (high + middle)[:, tokens:]
    first = high[:, tokens:]
    lane = lax.broadcasted_iota(jnp.int32, tail.shape, 1)
    gram = tail + pltpu.roll(both, 3 * rank, 1) + pltpu.roll(first, 2 * rank, 1)
    return total[:, :tokens], jnp.where(lane < rank, tail, gram)


def inverse_factors(gram_up, gram_down):
    rank = gram_up.shape[0]
    shape = (rank, 4 * rank)
    lane = lax.broadcasted_iota(jnp.int32, shape, 1)
    row = lax.broadcasted_iota(jnp.int32, shape, 0)
    part = lane // rank
    eye = ((lane - part * rank) == row).astype(F32)
    grams = jnp.where(part == 0, pltpu.roll(gram_up, 3 * rank, 1), pltpu.roll(gram_down, rank, 1))
    a = jnp.where((part == 0) | (part == 2), grams, eye)
    low = lane < 2 * rank
    for k in range(rank - 1):
        pivot_row = a[k : k + 1, :]
        column = jnp.where(low, a[:, k : k + 1], a[:, 2 * rank + k : 2 * rank + k + 1])
        pivot = jnp.where(
            low[:1], pivot_row[:, k : k + 1], pivot_row[:, 2 * rank + k : 2 * rank + k + 1]
        )
        scaled = pivot_row / pivot
        a = a - jnp.where(row > k, column, 0.0) * scaled
    diag_up = jnp.sum(jnp.where(lane == row, a, 0.0), axis=1, keepdims=True)
    diag_down = jnp.sum(jnp.where(lane == row + 2 * rank, a, 0.0), axis=1, keepdims=True)
    a = a / jnp.sqrt(jnp.where(low, diag_up, diag_down))
    return pltpu.roll(a, 3 * rank, 1)[:, :rank], pltpu.roll(a, rank, 1)[:, :rank]


def exchange_kernel(
    n_dp,
    n_mp,
    layer_in,
    up_grad,
    hidden,
    out_grad,
    eul,
    eur,
    edl,
    edr,
    q_up,
    q_down,
    q_up_out,
    q_down_out,
    a_up,
    b_up,
    a_down,
    b_down,
    pay_a,
    got_a,
    pay_b,
    got_b,
    work_p,
    core_p,
    right_p,
    left_p,
    full_p,
    work_q,
    core_q,
    right_q,
    left_q,
    full_q,
    p_block,
    q_block,
    mp_send,
    mp_recv,
    core_sem,
    line_send,
    line_recv,
    pair_send,
    pair_recv,
    block_send,
    block_recv,
):
    dp = lax.axis_index("dp")
    mp = lax.axis_index("mp")
    chips = n_dp // 2
    chip = dp // 2
    core = lax.rem(dp, 2)
    tokens = layer_in.shape[0]
    rank = eul.shape[0]
    small = layer_in.shape[1]
    small_pad = whole_tiles(small)
    large = hidden.shape[1]
    block = a_up.shape[1]
    per_shard = small // block
    owner = dp // per_shard
    half = core_p.shape[1]
    piece = half // (chips // 4)
    mate = (dp + 1 - 2 * core, mp)
    right = (dp + 2, mp)
    left = (dp - 2, mp)

    barrier = pltpu.get_barrier_semaphore()

    def greet(to):
        pl.semaphore_signal(barrier, inc=1, device_id=to, device_id_type=MESH)

    for j in range(1, n_mp):
        greet((dp, lax.rem(mp + j, n_mp)))
    greet(mate)

    @pl.when(chip > 0)
    def _():
        greet(left)

    @pl.when(chip < chips - 1)
    def _():
        greet(right)

    ends = jnp.where(chip > 0, 1, 0) + jnp.where(chip < chips - 1, 1, 0)
    pl.semaphore_wait(barrier, n_mp + ends)

    def remote(src, dst, send, recv, to):
        return pltpu.make_async_remote_copy(
            src_ref=src, dst_ref=dst, send_sem=send, recv_sem=recv, device_id=to, device_id_type=MESH
        )

    def sum_over_mp(pay, got, which):
        copies = []
        for j in range(1, n_mp):
            copies.append(
                remote(
                    pay,
                    got.at[j],
                    mp_send.at[which, j],
                    mp_recv.at[which, j],
                    (dp, lax.rem(mp + j, n_mp)),
                )
            )
            copies[-1].start()
        for c in copies:
            c.wait()
        got[0] = pay[...]
        total = got[lax.rem(mp, n_mp)]
        for i in range(1, n_mp):
            total = total + got[lax.rem(mp + n_mp - i, n_mp)]
        return total

    def all_reduce(work, pair, to_right, to_left, full, which):
        def at_piece(ref, s, base):
            rows = pl.ds(pl.multiple_of(8 * lax.rem(s, 4), 8), 8)
            return ref.at[rows, pl.ds(pl.multiple_of(base + (s // 4) * piece, LANES), piece)]

        mine = core * half
        theirs = (1 - core) * half
        swap = remote(
            work.at[:, pl.ds(pl.multiple_of(theirs, LANES), half)],
            pair,
            core_sem.at[which, 0],
            core_sem.at[which, 1],
            mate,
        )
        swap.start()
        swap.wait()

        own = pl.ds(pl.multiple_of(mine, LANES), half)
        pair[...] += work[:, own]

        def hop(buf, way, s, to):
            return remote(
                at_piece(buf, s, 0),
                at_piece(buf, s, 0),
                line_send.at[which, way, s],
                line_recv.at[which, way, s],
                to,
            )

        def hop_first(buf, way, s, to):
            return remote(
                at_piece(pair, s, 0),
                at_piece(buf, s, 0),
                line_send.at[which, way, s],
                line_recv.at[which, way, s],
                to,
            )

        def add_own(buf, s):
            at = at_piece(buf, s, 0)
            at[...] = at[...] + at_piece(pair, s, 0)[...]

        def reduce_step(k, carry):
            s = chips - 1 - k + chip

            @pl.when((k >= chip) & (chip < chips - 1))
            def _():
                @pl.when(chip > 0)
                def _():
                    hop(to_right, 0, s, right).wait_recv()
                    add_own(to_right, s)
                    hop(to_right, 0, s, right).start()

                @pl.when(chip == 0)
                def _():
                    hop_first(to_right, 0, s, right).start()

            z = k - (chips - 1 - chip)

            @pl.when((z >= 0) & (chip > 0))
            def _():
                @pl.when(chip < chips - 1)
                def _():
                    hop(to_left, 1, z, left).wait_recv()
                    add_own(to_left, z)
                    hop(to_left, 1, z, left).start()

                @pl.when(chip == chips - 1)
                def _():
                    hop_first(to_left, 1, z, left).start()

            return carry

        lax.fori_loop(0, chips - 1, reduce_step, 0)

        mine_here = at_piece(pair, chip, 0)

        @pl.when(chip > 0)
        def _():
            hop(to_right, 0, chip, right).wait_recv()
            mine_here[...] = mine_here[...] + at_piece(to_right, chip, 0)[...]

        @pl.when(chip < chips - 1)
        def _():
            hop(to_left, 1, chip, left).wait_recv()
            mine_here[...] = mine_here[...] + at_piece(to_left, chip, 0)[...]

        at_piece(full, chip, mine)[...] = mine_here[...] * (1.0 / n_dp)

        def spread(way, s, to):
            return remote(
                at_piece(full, s, mine),
                at_piece(full, s, mine),
                line_send.at[which, 2 + way, s],
                line_recv.at[which, 2 + way, s],
                to,
            )

        def to_mate(s):
            return remote(
                at_piece(full, s, mine),
                at_piece(full, s, mine),
                pair_send.at[which, s],
                pair_recv.at[which, s],
                mate,
            )

        def from_mate(s):
            return remote(
                at_piece(full, s, theirs),
                at_piece(full, s, theirs),
                pair_send.at[which, s],
                pair_recv.at[which, s],
                mate,
            )

        def spread_step(t, carry):
            s = chip - t

            @pl.when(s >= 0)
            def _():
                @pl.when(t > 0)
                def _():
                    spread(0, s, right).wait_recv()

                @pl.when(chip < chips - 1)
                def _():
                    spread(0, s, right).start()

            z = chip + t

            @pl.when(z < chips)
            def _():
                @pl.when(t > 0)
                def _():
                    spread(1, z, left).wait_recv()

                @pl.when(chip > 0)
                def _():
                    spread(1, z, left).start()

            @pl.when(s >= 0)
            def _():
                to_mate(s).start()

            @pl.when((z < chips) & (t > 0))
            def _():
                to_mate(z).start()

            return carry

        lax.fori_loop(0, chips, spread_step, 0)

        def drain(s, carry):
            from_mate(s).wait_recv()
            to_mate(s).wait_send()

            @pl.when(chip < s)
            def _():
                hop(to_right, 0, s, right).wait_send()

            @pl.when(chip > s)
            def _():
                hop(to_left, 1, s, left).wait_send()

            @pl.when((s <= chip) & (chip < chips - 1))
            def _():
                spread(0, s, right).wait_send()

            @pl.when((s >= chip) & (chip > 0))
            def _():
                spread(1, s, left).wait_send()

            return carry

        lax.fori_loop(0, chips, drain, 0)

    def send_block(buf, which):
        for j in range(1, n_mp):
            remote(
                buf, buf, block_send.at[which, j], block_recv.at[which], (dp, lax.rem(mp + j, n_mp))
            ).start()

    def wait_block(buf, which):
        @pl.when(mp == owner)
        def _():
            for j in range(1, n_mp):
                remote(
                    buf,
                    buf,
                    block_send.at[which, j],
                    block_recv.at[which],
                    (dp, lax.rem(mp + j, n_mp)),
                ).wait_send()

        @pl.when(mp != owner)
        def _():
            remote(
                buf, buf, block_send.at[which, 1], block_recv.at[which], (dp, lax.rem(mp + 1, n_mp))
            ).wait_recv()

    def pick_block(full, buf):
        shift = lax.rem(small_pad - lax.rem(dp, per_shard) * block, small_pad)
        rolled = pltpu.roll(full[:, :small_pad], shift, 1)
        buf[...] = rolled[:, : buf.shape[1]]

    pay_a[...] = jnp.zeros_like(pay_a)
    pay_a[0, :, : tokens + rank] = fold3(project(q_up, 0, up_grad, eur, False))
    pay_a[1, :, : tokens + rank] = fold3(project(q_down, 0, out_grad, edr, False))
    total = sum_over_mp(pay_a, got_a, 0)

    for work in (work_p, work_q):
        for a, b in ((small // LANES * LANES, small_pad), (small_pad + large, work.shape[1])):
            if b > a:
                work[:, a:b] = jnp.zeros((rank, b - a), F32)
    expand(total[0, :, : tokens + rank], layer_in, eul, work_p, 0)
    expand(total[1, :, : tokens + rank], hidden, edl, work_p, small_pad)
    all_reduce(work_p, core_p, right_p, left_p, full_p, 0)

    @pl.when(mp == owner)
    def _():
        pick_block(full_p, p_block)
        send_block(p_block, 0)

    for i, (start, rows, err) in enumerate(((0, layer_in, eul), (small_pad, hidden, edl))):
        first, second = gram_and_projections(project(full_p, start, rows, err, True), tokens)
        pay_b[i, :, :tokens] = first
        pay_b[i, :, tokens:] = second
    total = sum_over_mp(pay_b, got_b, 1)
    inv_up, inv_down = inverse_factors(total[0, :, tokens:], total[1, :, tokens:])
    t_up = dot_small(inv_up, total[0])[:, : tokens + rank]
    t_down = dot_small(inv_down, total[1])[:, : tokens + rank]
    expand(t_down, out_grad, edr, work_q, 0)
    expand(t_up, up_grad, eur, work_q, small_pad)
    all_reduce(work_q, core_q, right_q, left_q, full_q, 1)

    @pl.when(mp == owner)
    def _():
        pick_block(full_q, q_block)
        send_block(q_block, 1)

    q_down_out[...] = full_q[:, :small]

    def split_left(x):
        hi = x.astype(BF16)
        return jnp.concatenate([hi, hi, (x - hi.astype(F32)).astype(BF16)], axis=0)

    def split_right(x):
        hi = x.astype(BF16)
        return jnp.concatenate([hi, (x - hi.astype(F32)).astype(BF16), hi], axis=0)

    step = chunk_of(large)

    def finish(i, carry):
        at = pl.multiple_of(i * step, LANES)
        orth = dot_small(inv_down, full_p[:, pl.ds(small_pad + at, step)])
        b_down[:, pl.ds(at, step)] = split_right(orth)
        q = full_q[:, pl.ds(small_pad + at, step)]
        q_up_out[:, pl.ds(at, step)] = q
        b_up[:, pl.ds(at, step)] = split_right(q)
        return carry

    lax.fori_loop(0, large // step, finish, 0)

    wait_block(p_block, 0)
    a_up[...] = split_left(dot_small(inv_up, p_block[...]))[:, :block]
    wait_block(q_block, 1)
    a_down[...] = split_left(q_block[...])[:, :block]


def momentum_kernel(m_up, m_down, a_up, b_up, a_down, b_down, out_up, out_down):
    for m, a, b, out in ((m_up, a_up, b_up, out_up), (m_down, a_down, b_down, out_down)):
        delta = lax.dot_general(
            a[...], b[...], (((0,), (0,)), ((), ())), preferred_element_type=F32
        )
        out[...] = (0.9 * m[...].astype(F32) + delta).astype(BF16)


def on_device(
    layer_in,
    up_grad,
    hidden,
    out_grad,
    err_up_left,
    err_up_right,
    err_down_left,
    err_down_right,
    q_up,
    q_down,
    momentum_up,
    momentum_down,
):
    n_dp = lax.axis_size("dp")
    n_mp = lax.axis_size("mp")
    chips = n_dp // 2
    tokens, small = layer_in.shape
    large = hidden.shape[1]
    rank = q_up.shape[1]
    block = momentum_up.shape[0]
    block_pad = whole_tiles(block)
    pieces = n_dp // 4
    piece = -(-((whole_tiles(small) + large) // LANES) // pieces) * LANES
    half = piece * pieces // 2
    vmem = pl.BlockSpec(memory_space=pltpu.VMEM)
    dma = pltpu.SemaphoreType.DMA
    reduce_buffers = [
        pltpu.VMEM((rank, 2 * half), F32),
        pltpu.VMEM((rank, half), F32),
        pltpu.VMEM((rank, half), F32),
        pltpu.VMEM((rank, half), F32),
        pltpu.VMEM((rank, 2 * half), F32),
    ]
    pay = pltpu.VMEM((2, rank, tokens + 4 * rank), F32)
    got = pltpu.VMEM((n_mp, 2, rank, tokens + 4 * rank), F32)
    q_up_t, q_down_t, a_up, b_up, a_down, b_down = pl.pallas_call(
        functools.partial(exchange_kernel, n_dp, n_mp),
        out_shape=(
            jax.ShapeDtypeStruct((rank, large), F32),
            jax.ShapeDtypeStruct((rank, small), F32),
            jax.ShapeDtypeStruct((3 * rank, block), BF16),
            jax.ShapeDtypeStruct((3 * rank, large), BF16),
            jax.ShapeDtypeStruct((3 * rank, block), BF16),
            jax.ShapeDtypeStruct((3 * rank, large), BF16),
        ),
        in_specs=[vmem] * 10,
        out_specs=[vmem] * 6,
        scratch_shapes=[
            pay,
            got,
            pay,
            got,
            *reduce_buffers,
            *reduce_buffers,
            pltpu.VMEM((rank, block_pad), F32),
            pltpu.VMEM((rank, block_pad), F32),
            dma((2, n_mp)),
            dma((2, n_mp)),
            dma((2, 2)),
            dma((2, 4, chips)),
            dma((2, 4, chips)),
            dma((2, chips)),
            dma((2, chips)),
            dma((2, n_mp)),
            dma((2,)),
        ],
        compiler_params=pltpu.CompilerParams(
            collective_id=0, has_side_effects=True, vmem_limit_bytes=30 * 1024 * 1024
        ),
    )(
        layer_in,
        up_grad,
        hidden,
        out_grad,
        err_up_left[0].T,
        err_up_right[0].T,
        err_down_left[0].T,
        err_down_right[0].T,
        q_up.T,
        q_down.T,
    )
    step = chunk_of(large)
    wide = pl.BlockSpec((block, step), lambda i: (0, i))
    left = pl.BlockSpec((3 * rank, block), lambda i: (0, 0))
    right = pl.BlockSpec((3 * rank, step), lambda i: (0, i))
    new_up, new_down_t = pl.pallas_call(
        momentum_kernel,
        grid=(large // step,),
        out_shape=(
            jax.ShapeDtypeStruct((block, large), BF16),
            jax.ShapeDtypeStruct((block, large), BF16),
        ),
        in_specs=[wide, wide, left, right, left, right],
        out_specs=[wide, wide],
        compiler_params=pltpu.CompilerParams(vmem_limit_bytes=32 * 1024 * 1024),
    )(momentum_up, momentum_down.T, a_up, b_up, a_down, b_down)
    return (q_up_t.T, q_down_t.T, new_up, new_down_t.T)


def solution(mesh):
    return jax.shard_map(
        on_device,
        mesh=mesh,
        in_specs=(
            P("dp", "mp"),
            P("dp", "mp"),
            P("dp", "mp"),
            P("dp", "mp"),
            P("dp", "mp", None),
            P("dp", "mp", None),
            P("dp", "mp", None),
            P("dp", "mp", None),
            P("mp", None),
            P("mp", None),
            P("dp", "mp"),
            P("mp", "dp"),
        ),
        out_specs=(P("mp", None), P("mp", None), P("dp", "mp"), P("mp", "dp")),
        check_vma=False,
    )
```

```python
import functools

import jax
import jax.numpy as jnp
from jax import lax
from jax.experimental import pallas as pl
from jax.experimental.pallas import tpu as pltpu
from jax.sharding import PartitionSpec as P

F32 = jnp.float32
BF16 = jnp.bfloat16
MESH = pl.DeviceIdType.MESH
LANES = 128
MAX_CHUNK = 1152


def whole_tiles(width):
    return -(-width // LANES) * LANES


def chunk_of(width):
    if width % LANES:
        return width
    size = MAX_CHUNK
    while width % size:
        size -= LANES
    return size


def split3(x):
    hi = x.astype(BF16)
    rest = x - hi.astype(F32)
    mid = rest.astype(BF16)
    lo = (rest - mid.astype(F32)).astype(BF16)
    return jnp.concatenate([hi, mid, lo], axis=0)


def fold3(x):
    rank = x.shape[0] // 3
    return x[:rank] + x[rank : 2 * rank] + x[2 * rank :]


def dot_nt(a, b):
    return lax.dot_general(a, b, (((1,), (1,)), ((), ())), preferred_element_type=F32)


def dot_nn(a, b):
    return jnp.dot(a, b, preferred_element_type=F32)


def dot_small(a, b):
    return jnp.dot(a, b, precision=lax.Precision.HIGHEST, preferred_element_type=F32)


def project(x_ref, start, rows_ref, err_ref, with_gram):
    width = rows_ref.shape[1]
    step = chunk_of(width)
    outs = rows_ref.shape[0] + err_ref.shape[0] + (3 * err_ref.shape[0] if with_gram else 0)

    def body(i, acc):
        at = 0 if step == width else pl.multiple_of(i * step, LANES)
        x = split3(x_ref[:, pl.ds(start + at, step)])
        parts = [rows_ref[:, pl.ds(at, step)], err_ref[:, pl.ds(at, step)]]
        if with_gram:
            parts.append(x)
        return acc + dot_nt(x, jnp.concatenate(parts, axis=0))

    zero = jnp.zeros((3 * err_ref.shape[0], outs), F32)
    return body(0, zero) if step == width else lax.fori_loop(0, width // step, body, zero)


def expand(left, rows_ref, err_ref, out_ref, start):
    width = rows_ref.shape[1]
    step = chunk_of(width)
    stacked = split3(left)

    def body(i, carry):
        at = 0 if step == width else pl.multiple_of(i * step, LANES)
        right = jnp.concatenate([rows_ref[:, pl.ds(at, step)], err_ref[:, pl.ds(at, step)]], axis=0)
        out_ref[:, pl.ds(start + at, step)] = fold3(dot_nn(stacked, right))
        return carry

    if step == width:
        body(0, 0)
    else:
        lax.fori_loop(0, width // step, body, 0)


def gram_and_projections(acc, tokens):
    rank = acc.shape[0] // 3
    high, middle = acc[:rank], acc[rank : 2 * rank]
    low = acc[2 * rank :]
    total = high + middle + low
    tail = total[:, tokens:]
    both = (high + middle)[:, tokens:]
    first = high[:, tokens:]
    lane = lax.broadcasted_iota(jnp.int32, tail.shape, 1)
    gram = tail + pltpu.roll(both, 3 * rank, 1) + pltpu.roll(first, 2 * rank, 1)
    return total[:, :tokens], jnp.where(lane < rank, tail, gram)


def inverse_factors(gram_up, gram_down):
    rank = gram_up.shape[0]
    shape = (rank, 4 * rank)
    lane = lax.broadcasted_iota(jnp.int32, shape, 1)
    row = lax.broadcasted_iota(jnp.int32, shape, 0)
    part = lane // rank
    eye = ((lane - part * rank) == row).astype(F32)
    grams = jnp.where(part == 0, pltpu.roll(gram_up, 3 * rank, 1), pltpu.roll(gram_down, rank, 1))
    a = jnp.where((part == 0) | (part == 2), grams, eye)
    low = lane < 2 * rank
    for k in range(rank - 1):
        pivot_row = a[k : k + 1, :]
        column = jnp.where(low, a[:, k : k + 1], a[:, 2 * rank + k : 2 * rank + k + 1])
        pivot = jnp.where(
            low[:1], pivot_row[:, k : k + 1], pivot_row[:, 2 * rank + k : 2 * rank + k + 1]
        )
        scaled = pivot_row / pivot
        a = a - jnp.where(row > k, column, 0.0) * scaled
    diag_up = jnp.sum(jnp.where(lane == row, a, 0.0), axis=1, keepdims=True)
    diag_down = jnp.sum(jnp.where(lane == row + 2 * rank, a, 0.0), axis=1, keepdims=True)
    a = a / jnp.sqrt(jnp.where(low, diag_up, diag_down))
    return pltpu.roll(a, 3 * rank, 1)[:, :rank], pltpu.roll(a, rank, 1)[:, :rank]


def exchange_kernel(
    n_dp,
    n_mp,
    *refs,
):
    operands, outputs, held = refs[:12], refs[12:18], refs[18:28]
    full_q, m_up, m_down, b_down, a_up, q_block = outputs
    (
        pay_a,
        got_a,
        pay_b,
        got_b,
        work_p,
        pair_p,
        right_p,
        left_p,
        full_p,
        work_q,
        pair_q,
        right_q,
        left_q,
        p_block,
        load_sem,
        mp_send,
        mp_recv,
        swap_send,
        swap_recv,
        line_send,
        line_recv,
        mate_send,
        mate_recv,
        block_send,
        block_recv,
    ) = refs[28:]
    layer_in, up_grad, hidden, out_grad, eul, eur, edl, edr, q_up, q_down = held
    landing = (*held, m_up, m_down)
    loads = [pltpu.make_async_copy(operands[i], landing[i], load_sem.at[i]) for i in range(12)]
    first_loads, second_loads, last_loads = (8, 1, 5, 9, 3, 7), (0, 4, 2, 6), (10, 11)
    for i in first_loads + second_loads + last_loads:
        loads[i].start()
    dp = lax.axis_index("dp")
    mp = lax.axis_index("mp")
    chips = n_dp // 2
    chip = dp // 2
    core = lax.rem(dp, 2)
    tokens = layer_in.shape[0]
    rank = eul.shape[0]
    small = layer_in.shape[1]
    small_pad = whole_tiles(small)
    large = hidden.shape[1]
    block = m_up.shape[0]
    per_shard = small // block
    owner = dp // per_shard
    half = pair_p.shape[1]
    piece = half // (chips // 4)
    mate = (dp + 1 - 2 * core, mp)
    right = (dp + 2, mp)
    left = (dp - 2, mp)

    barrier = pltpu.get_barrier_semaphore()

    def greet(to):
        pl.semaphore_signal(barrier, inc=1, device_id=to, device_id_type=MESH)

    for j in range(1, n_mp):
        greet((dp, lax.rem(mp + j, n_mp)))
    greet(mate)

    @pl.when(chip > 0)
    def _():
        greet(left)

    @pl.when(chip < chips - 1)
    def _():
        greet(right)

    ends = jnp.where(chip > 0, 1, 0) + jnp.where(chip < chips - 1, 1, 0)
    pl.semaphore_wait(barrier, n_mp + ends)

    def remote(src, dst, send, recv, to):
        return pltpu.make_async_remote_copy(
            src_ref=src, dst_ref=dst, send_sem=send, recv_sem=recv, device_id=to, device_id_type=MESH
        )

    def sum_over_mp(pay, got, which):
        copies = []
        for j in range(1, n_mp):
            copies.append(
                remote(
                    pay,
                    got.at[j],
                    mp_send.at[which, j],
                    mp_recv.at[which, j],
                    (dp, lax.rem(mp + j, n_mp)),
                )
            )
            copies[-1].start()
        for c in copies:
            c.wait()
        got[0] = pay[...]
        total = got[lax.rem(mp, n_mp)]
        for i in range(1, n_mp):
            total = total + got[lax.rem(mp + n_mp - i, n_mp)]
        return total

    def all_reduce(work, pair, to_right, to_left, full, which, meanwhile):
        def at_piece(ref, s, base):
            rows = pl.ds(pl.multiple_of(8 * lax.rem(s, 4), 8), 8)
            return ref.at[rows, pl.ds(pl.multiple_of(base + (s // 4) * piece, LANES), piece)]

        mine = core * half
        theirs = (1 - core) * half

        def swap(s):
            return remote(
                at_piece(work, s, theirs),
                at_piece(pair, s, 0),
                swap_send.at[which, s],
                swap_recv.at[which, s],
                mate,
            )

        def start_swap(t, carry):
            swap(jnp.where(lax.rem(t, 2) == 0, chips - 1 - t // 2, t // 2)).start()
            return carry

        lax.fori_loop(0, chips, start_swap, 0)

        def add_mate(s):
            swap(s).wait_recv()
            at = at_piece(pair, s, 0)
            at[...] = at[...] + at_piece(work, s, mine)[...]

        def hop(buf, way, s, to):
            return remote(
                at_piece(buf, s, 0),
                at_piece(buf, s, 0),
                line_send.at[which, way, s],
                line_recv.at[which, way, s],
                to,
            )

        def hop_first(buf, way, s, to):
            return remote(
                at_piece(pair, s, 0),
                at_piece(buf, s, 0),
                line_send.at[which, way, s],
                line_recv.at[which, way, s],
                to,
            )

        def add_own(buf, s):
            at = at_piece(buf, s, 0)
            at[...] = at[...] + at_piece(pair, s, 0)[...]

        def reduce_step(k, carry):
            s = chips - 1 - k + chip

            @pl.when((k >= chip) & (chip < chips - 1))
            def _():
                add_mate(s)

                @pl.when(chip > 0)
                def _():
                    hop(to_right, 0, s, right).wait_recv()
                    add_own(to_right, s)
                    hop(to_right, 0, s, right).start()

                @pl.when(chip == 0)
                def _():
                    hop_first(to_right, 0, s, right).start()

            z = k - (chips - 1 - chip)

            @pl.when((z >= 0) & (chip > 0))
            def _():
                add_mate(z)

                @pl.when(chip < chips - 1)
                def _():
                    hop(to_left, 1, z, left).wait_recv()
                    add_own(to_left, z)
                    hop(to_left, 1, z, left).start()

                @pl.when(chip == chips - 1)
                def _():
                    hop_first(to_left, 1, z, left).start()

            return carry

        reduce_step(0, 0)
        meanwhile()
        lax.fori_loop(1, chips - 1, reduce_step, 0)
        add_mate(chip)

        mine_here = at_piece(pair, chip, 0)

        @pl.when(chip > 0)
        def _():
            hop(to_right, 0, chip, right).wait_recv()
            mine_here[...] = mine_here[...] + at_piece(to_right, chip, 0)[...]

        @pl.when(chip < chips - 1)
        def _():
            hop(to_left, 1, chip, left).wait_recv()
            mine_here[...] = mine_here[...] + at_piece(to_left, chip, 0)[...]

        at_piece(full, chip, mine)[...] = mine_here[...] * (1.0 / n_dp)

        def spread(way, s, to):
            return remote(
                at_piece(full, s, mine),
                at_piece(full, s, mine),
                line_send.at[which, 2 + way, s],
                line_recv.at[which, 2 + way, s],
                to,
            )

        def to_mate(s):
            return remote(
                at_piece(full, s, mine),
                at_piece(full, s, mine),
                mate_send.at[which, s],
                mate_recv.at[which, s],
                mate,
            )

        def from_mate(s):
            return remote(
                at_piece(full, s, theirs),
                at_piece(full, s, theirs),
                mate_send.at[which, s],
                mate_recv.at[which, s],
                mate,
            )

        def spread_step(t, carry):
            s = chip - t

            @pl.when(s >= 0)
            def _():
                @pl.when(t > 0)
                def _():
                    spread(0, s, right).wait_recv()

                @pl.when(chip < chips - 1)
                def _():
                    spread(0, s, right).start()

            z = chip + t

            @pl.when(z < chips)
            def _():
                @pl.when(t > 0)
                def _():
                    spread(1, z, left).wait_recv()

                @pl.when(chip > 0)
                def _():
                    spread(1, z, left).start()

            @pl.when(s >= 0)
            def _():
                to_mate(s).start()

            @pl.when((z < chips) & (t > 0))
            def _():
                to_mate(z).start()

            return carry

        lax.fori_loop(0, chips, spread_step, 0)

        def drain(s, carry):
            from_mate(s).wait_recv()
            swap(s).wait_send()
            to_mate(s).wait_send()

            @pl.when(chip < s)
            def _():
                hop(to_right, 0, s, right).wait_send()

            @pl.when(chip > s)
            def _():
                hop(to_left, 1, s, left).wait_send()

            @pl.when((s <= chip) & (chip < chips - 1))
            def _():
                spread(0, s, right).wait_send()

            @pl.when((s >= chip) & (chip > 0))
            def _():
                spread(1, s, left).wait_send()

            return carry

        lax.fori_loop(0, chips, drain, 0)

    def send_block(buf, which):
        for j in range(1, n_mp):
            remote(
                buf, buf, block_send.at[which, j], block_recv.at[which], (dp, lax.rem(mp + j, n_mp))
            ).start()

    def wait_block(buf, which):
        @pl.when(mp == owner)
        def _():
            for j in range(1, n_mp):
                remote(
                    buf,
                    buf,
                    block_send.at[which, j],
                    block_recv.at[which],
                    (dp, lax.rem(mp + j, n_mp)),
                ).wait_send()

        @pl.when(mp != owner)
        def _():
            remote(
                buf, buf, block_send.at[which, 1], block_recv.at[which], (dp, lax.rem(mp + 1, n_mp))
            ).wait_recv()

    def pick_block(full, buf):
        shift = lax.rem(small_pad - lax.rem(dp, per_shard) * block, small_pad)
        rolled = pltpu.roll(full[:, :small_pad], shift, 1)
        buf[...] = rolled[:, : buf.shape[1]]

    for i in first_loads:
        loads[i].wait()
    pay_a[...] = jnp.zeros_like(pay_a)
    pay_a[0, :, : tokens + rank] = fold3(project(q_up, 0, up_grad, eur, False))
    pay_a[1, :, : tokens + rank] = fold3(project(q_down, 0, out_grad, edr, False))
    total = sum_over_mp(pay_a, got_a, 0)

    for work in (work_p, work_q):
        for a, b in ((small // LANES * LANES, small_pad), (small_pad + large, work.shape[1])):
            if b > a:
                work[:, a:b] = jnp.zeros((rank, b - a), F32)
    for i in second_loads:
        loads[i].wait()
    expand(total[0, :, : tokens + rank], layer_in, eul, work_p, 0)
    expand(total[1, :, : tokens + rank], hidden, edl, work_p, small_pad)
    all_reduce(work_p, pair_p, right_p, left_p, full_p, 0, lambda: None)

    @pl.when(mp == owner)
    def _():
        pick_block(full_p, p_block)
        send_block(p_block, 0)

    for i, (start, rows, err) in enumerate(((0, layer_in, eul), (small_pad, hidden, edl))):
        first, second = gram_and_projections(project(full_p, start, rows, err, True), tokens)
        pay_b[i, :, :tokens] = first
        pay_b[i, :, tokens:] = second
    total = sum_over_mp(pay_b, got_b, 1)
    inv_up, inv_down = inverse_factors(total[0, :, tokens:], total[1, :, tokens:])
    t_up = dot_small(inv_up, total[0])[:, : tokens + rank]
    t_down = dot_small(inv_down, total[1])[:, : tokens + rank]
    expand(t_down, out_grad, edr, work_q, 0)
    expand(t_up, up_grad, eur, work_q, small_pad)

    def orthonormal():
        step = chunk_of(large)

        def body(i, carry):
            at = pl.multiple_of(i * step, LANES)
            orth = dot_small(inv_down, full_p[:, pl.ds(small_pad + at, step)])
            b_down[:, pl.ds(at, step)] = split_right(orth)
            return carry

        lax.fori_loop(0, large // step, body, 0)

    all_reduce(work_q, pair_q, right_q, left_q, full_q, 1, orthonormal)

    @pl.when(mp == owner)
    def _():
        pick_block(full_q, q_block)
        send_block(q_block, 1)

    wait_block(p_block, 0)
    a_up[...] = dot_small(inv_up, p_block[...])
    for i in last_loads:
        loads[i].wait()
    wait_block(q_block, 1)


def split_right(x):
    hi = x.astype(BF16)
    return jnp.concatenate([hi, (x - hi.astype(F32)).astype(BF16), hi], axis=0)


def split_left(x):
    hi = x.astype(BF16).astype(F32)
    return jnp.concatenate([hi, hi, x - hi], axis=0).T.astype(BF16)


def momentum_kernel(
    small,
    full_q,
    m_up,
    m_down,
    b_down,
    a_up,
    a_down,
    q_up_out,
    q_down_out,
    out_up,
    out_down,
    buf_up,
    buf_down,
    left_up,
    left_down,
    q_small,
    sem_up,
    sem_down,
    sem_q,
):
    block, large = m_up.shape
    step = buf_up.shape[2]
    start = whole_tiles(small)
    q_small[...] = full_q[:, :small]
    q_copies = (
        pltpu.make_async_copy(full_q.at[:, pl.ds(start, large)], q_up_out, sem_q.at[0]),
        pltpu.make_async_copy(q_small, q_down_out, sem_q.at[1]),
    )
    left_up[...] = split_left(a_up[...])[:block]
    left_down[...] = split_left(a_down[...])[:block]

    def copy(buf, out, sem, i):
        columns = pl.ds(pl.multiple_of(i * step, LANES), step)
        return pltpu.make_async_copy(buf.at[i % 2], out.at[:, columns], sem.at[i % 2])

    def body(i, carry):
        at = pl.multiple_of(i * step, LANES)
        columns = pl.ds(at, step)
        q = split_right(full_q[:, pl.ds(start + at, step)])
        for m, a, b, buf, out, sem in (
            (m_up, left_up, q, buf_up, out_up, sem_up),
            (m_down, left_down, b_down[:, columns], buf_down, out_down, sem_down),
        ):

            @pl.when(i >= 2)
            def _():
                copy(buf, out, sem, i - 2).wait()

            delta = dot_nn(a[...], b)
            buf[i % 2] = (0.9 * m[:, columns].astype(F32) + delta).astype(BF16)
            copy(buf, out, sem, i).start()
        return carry

    count = large // step
    lax.fori_loop(0, count, body, 0)
    for c in q_copies:
        c.start()
    for i in range(max(count - 2, 0), count):
        copy(buf_up, out_up, sem_up, i).wait()
        copy(buf_down, out_down, sem_down, i).wait()
    for c in q_copies:
        c.wait()


def on_device(
    layer_in,
    up_grad,
    hidden,
    out_grad,
    err_up_left,
    err_up_right,
    err_down_left,
    err_down_right,
    q_up,
    q_down,
    momentum_up,
    momentum_down,
):
    n_dp = lax.axis_size("dp")
    n_mp = lax.axis_size("mp")
    chips = n_dp // 2
    tokens, small = layer_in.shape
    large = hidden.shape[1]
    rank = q_up.shape[1]
    block = momentum_up.shape[0]
    block_pad = whole_tiles(block)
    pieces = n_dp // 4
    piece = -(-((whole_tiles(small) + large) // LANES) // pieces) * LANES
    half = piece * pieces // 2
    vmem = pl.BlockSpec(memory_space=pltpu.VMEM)
    hbm = pl.BlockSpec(memory_space=pltpu.HBM)
    dma = pltpu.SemaphoreType.DMA
    operands = (
        layer_in,
        up_grad,
        hidden,
        out_grad,
        err_up_left[0].T,
        err_up_right[0].T,
        err_down_left[0].T,
        err_down_right[0].T,
        q_up.T,
        q_down.T,
        momentum_up,
        momentum_down.T,
    )
    operands = tuple(pltpu.with_memory_space_constraint(x, pltpu.HBM) for x in operands)
    whole = pltpu.VMEM((rank, 2 * half), F32)
    part = pltpu.VMEM((rank, half), F32)
    pay = pltpu.VMEM((2, rank, tokens + 4 * rank), F32)
    got = pltpu.VMEM((n_mp, 2, rank, tokens + 4 * rank), F32)
    full_q, m_up, m_down, b_down, a_up, a_down = pl.pallas_call(
        functools.partial(exchange_kernel, n_dp, n_mp),
        out_shape=(
            jax.ShapeDtypeStruct((rank, 2 * half), F32),
            jax.ShapeDtypeStruct((block, large), BF16),
            jax.ShapeDtypeStruct((block, large), BF16),
            jax.ShapeDtypeStruct((3 * rank, large), BF16),
            jax.ShapeDtypeStruct((rank, block_pad), F32),
            jax.ShapeDtypeStruct((rank, block_pad), F32),
        ),
        in_specs=[hbm] * 12,
        out_specs=[vmem] * 6,
        scratch_shapes=[
            *[pltpu.VMEM(x.shape, x.dtype) for x in operands[:10]],
            pay,
            got,
            pay,
            got,
            *[whole, part, part, part, whole],
            *[whole, part, part, part],
            pltpu.VMEM((rank, block_pad), F32),
            dma((12,)),
            dma((2, n_mp)),
            dma((2, n_mp)),
            dma((2, chips)),
            dma((2, chips)),
            dma((2, 4, chips)),
            dma((2, 4, chips)),
            dma((2, chips)),
            dma((2, chips)),
            dma((2, n_mp)),
            dma((2,)),
        ],
        compiler_params=pltpu.CompilerParams(
            collective_id=0, has_side_effects=True, vmem_limit_bytes=26 * 1024 * 1024
        ),
    )(*operands)
    step = chunk_of(large)
    slots = pltpu.VMEM((2, block, step), BF16)
    left = pltpu.VMEM((block, 3 * rank), BF16)
    q_up_t, q_down_t, new_up, new_down_t = pl.pallas_call(
        functools.partial(momentum_kernel, small),
        out_shape=(
            jax.ShapeDtypeStruct((rank, large), F32),
            jax.ShapeDtypeStruct((rank, small), F32),
            jax.ShapeDtypeStruct((block, large), BF16),
            jax.ShapeDtypeStruct((block, large), BF16),
        ),
        in_specs=[vmem] * 6,
        out_specs=[hbm] * 4,
        scratch_shapes=[
            slots,
            slots,
            left,
            left,
            pltpu.VMEM((rank, small), F32),
            dma((2,)),
            dma((2,)),
            dma((2,)),
        ],
        compiler_params=pltpu.CompilerParams(vmem_limit_bytes=16 * 1024 * 1024),
    )(full_q, m_up, m_down, b_down, a_up, a_down)
    return (q_up_t.T, q_down_t.T, new_up, new_down_t.T)


def solution(mesh):
    return jax.shard_map(
        on_device,
        mesh=mesh,
        in_specs=(
            P("dp", "mp"),
            P("dp", "mp"),
            P("dp", "mp"),
            P("dp", "mp"),
            P("dp", "mp", None),
            P("dp", "mp", None),
            P("dp", "mp", None),
            P("dp", "mp", None),
            P("mp", None),
            P("mp", None),
            P("dp", "mp"),
            P("mp", "dp"),
        ),
        out_specs=(P("mp", None), P("mp", None), P("dp", "mp"), P("mp", "dp")),
        check_vma=False,
    )
```

```python
import functools

import jax
import jax.numpy as jnp
from jax import lax
from jax.experimental import pallas as pl
from jax.experimental.pallas import tpu as pltpu
from jax.sharding import PartitionSpec as P

F32 = jnp.float32
BF16 = jnp.bfloat16
MESH = pl.DeviceIdType.MESH
LANES = 128
MAX_CHUNK = 1152


def whole_tiles(width):
    return -(-width // LANES) * LANES


def chunk_of(width):
    if width % LANES:
        return width
    size = MAX_CHUNK
    while width % size:
        size -= LANES
    return size


def split3(x):
    hi = x.astype(BF16)
    rest = x - hi.astype(F32)
    mid = rest.astype(BF16)
    lo = (rest - mid.astype(F32)).astype(BF16)
    return jnp.concatenate([hi, mid, lo], axis=0)


def fold3(x):
    rank = x.shape[0] // 3
    return x[:rank] + x[rank : 2 * rank] + x[2 * rank :]


def dot_nt(a, b):
    return lax.dot_general(a, b, (((1,), (1,)), ((), ())), preferred_element_type=F32)


def dot_nn(a, b):
    return jnp.dot(a, b, preferred_element_type=F32)


def dot_small(a, b):
    return jnp.dot(a, b, precision=lax.Precision.HIGHEST, preferred_element_type=F32)


def project(x_ref, start, rows_ref, err_ref, with_gram):
    width = rows_ref.shape[1]
    step = chunk_of(width)
    outs = rows_ref.shape[0] + err_ref.shape[0] + (3 * err_ref.shape[0] if with_gram else 0)

    def body(i, acc):
        at = 0 if step == width else pl.multiple_of(i * step, LANES)
        x = split3(x_ref[:, pl.ds(start + at, step)])
        parts = [rows_ref[:, pl.ds(at, step)], err_ref[:, pl.ds(at, step)]]
        if with_gram:
            parts.append(x)
        return acc + dot_nt(x, jnp.concatenate(parts, axis=0))

    zero = jnp.zeros((3 * err_ref.shape[0], outs), F32)
    return body(0, zero) if step == width else lax.fori_loop(0, width // step, body, zero, unroll=True)


def expand(left, rows_ref, err_ref, out_ref, start):
    width = rows_ref.shape[1]
    step = chunk_of(width)
    stacked = split3(left)

    def body(i, carry):
        at = 0 if step == width else pl.multiple_of(i * step, LANES)
        right = jnp.concatenate([rows_ref[:, pl.ds(at, step)], err_ref[:, pl.ds(at, step)]], axis=0)
        out_ref[:, pl.ds(start + at, step)] = fold3(dot_nn(stacked, right))
        return carry

    if step == width:
        body(0, 0)
    else:
        lax.fori_loop(0, width // step, body, 0, unroll=True)


def gram_and_projections(acc, tokens):
    rank = acc.shape[0] // 3
    high, middle = acc[:rank], acc[rank : 2 * rank]
    low = acc[2 * rank :]
    total = high + middle + low
    tail = total[:, tokens:]
    both = (high + middle)[:, tokens:]
    first = high[:, tokens:]
    lane = lax.broadcasted_iota(jnp.int32, tail.shape, 1)
    gram = tail + pltpu.roll(both, 3 * rank, 1) + pltpu.roll(first, 2 * rank, 1)
    return total[:, :tokens], jnp.where(lane < rank, tail, gram)


def inverse_factors(gram_up, gram_down):
    rank = gram_up.shape[0]
    shape = (rank, 4 * rank)
    lane = lax.broadcasted_iota(jnp.int32, shape, 1)
    row = lax.broadcasted_iota(jnp.int32, shape, 0)
    part = lane // rank
    eye = ((lane - part * rank) == row).astype(F32)
    grams = jnp.where(part == 0, pltpu.roll(gram_up, 3 * rank, 1), pltpu.roll(gram_down, rank, 1))
    a = jnp.where((part == 0) | (part == 2), grams, eye)
    low = lane < 2 * rank
    for k in range(rank - 1):
        pivot_row = a[k : k + 1, :]
        column = jnp.where(low, a[:, k : k + 1], a[:, 2 * rank + k : 2 * rank + k + 1])
        scaled = pivot_row / column[k : k + 1, :]
        a = a - jnp.where(row > k, column, 0.0) * scaled
    diag_up = jnp.sum(jnp.where(lane == row, a, 0.0), axis=1, keepdims=True)
    diag_down = jnp.sum(jnp.where(lane == row + 2 * rank, a, 0.0), axis=1, keepdims=True)
    a = a / jnp.sqrt(jnp.where(low, diag_up, diag_down))
    return pltpu.roll(a, 3 * rank, 1)[:, :rank], pltpu.roll(a, rank, 1)[:, :rank]


def exchange_kernel(
    n_dp,
    n_mp,
    *refs,
):
    operands, outputs, held = refs[:12], refs[12:18], refs[18:28]
    full_q, m_up, m_down, b_down, a_up, q_block = outputs
    (
        pay_a,
        got_a,
        pay_b,
        got_b,
        work_p,
        pair_p,
        right_p,
        left_p,
        full_p,
        work_q,
        pair_q,
        right_q,
        left_q,
        p_block,
        load_sem,
        mp_send,
        mp_recv,
        swap_send,
        swap_recv,
        line_send,
        line_recv,
        mate_send,
        mate_recv,
        block_send,
        block_recv,
    ) = refs[28:]
    layer_in, up_grad, hidden, out_grad, eul, eur, edl, edr, q_up, q_down = held
    landing = (*held, m_up, m_down)
    loads = [pltpu.make_async_copy(operands[i], landing[i], load_sem.at[i]) for i in range(12)]
    first_loads, second_loads, last_loads = (8, 1, 5, 9, 3, 7), (0, 4, 2, 6), (10, 11)
    for i in first_loads + second_loads + last_loads:
        loads[i].start()
    dp = lax.axis_index("dp")
    mp = lax.axis_index("mp")
    chips = n_dp // 2
    chip = dp // 2
    core = lax.rem(dp, 2)
    tokens = layer_in.shape[0]
    rank = eul.shape[0]
    small = layer_in.shape[1]
    small_pad = whole_tiles(small)
    large = hidden.shape[1]
    block = m_up.shape[0]
    per_shard = small // block
    owner = dp // per_shard
    half = pair_p.shape[1]
    piece = half // (chips // 4)
    mate = (dp + 1 - 2 * core, mp)
    right = (dp + 2, mp)
    left = (dp - 2, mp)

    barrier = pltpu.get_barrier_semaphore()

    def greet(to):
        pl.semaphore_signal(barrier, inc=1, device_id=to, device_id_type=MESH)

    for j in range(1, n_mp):
        greet((dp, lax.rem(mp + j, n_mp)))
    greet(mate)

    @pl.when(chip > 0)
    def _():
        greet(left)

    @pl.when(chip < chips - 1)
    def _():
        greet(right)

    ends = jnp.where(chip > 0, 1, 0) + jnp.where(chip < chips - 1, 1, 0)
    pl.semaphore_wait(barrier, n_mp + ends)

    def remote(src, dst, send, recv, to):
        return pltpu.make_async_remote_copy(
            src_ref=src, dst_ref=dst, send_sem=send, recv_sem=recv, device_id=to, device_id_type=MESH
        )

    def sum_over_mp(pay, got, which):
        copies = []
        for j in range(1, n_mp):
            copies.append(
                remote(
                    pay,
                    got.at[j],
                    mp_send.at[which, j],
                    mp_recv.at[which, j],
                    (dp, lax.rem(mp + j, n_mp)),
                )
            )
            copies[-1].start()
        for c in copies:
            c.wait()
        got[0] = pay[...]
        total = got[lax.rem(mp, n_mp)]
        for i in range(1, n_mp):
            total = total + got[lax.rem(mp + n_mp - i, n_mp)]
        return total

    def all_reduce(work, pair, to_right, to_left, full, which, meanwhile):
        def at_piece(ref, s, base):
            rows = pl.ds(pl.multiple_of(8 * lax.rem(s, 4), 8), 8)
            return ref.at[rows, pl.ds(pl.multiple_of(base + (s // 4) * piece, LANES), piece)]

        mine = core * half
        theirs = (1 - core) * half

        def swap(s):
            return remote(
                at_piece(work, s, theirs),
                at_piece(pair, s, 0),
                swap_send.at[which, s],
                swap_recv.at[which, s],
                mate,
            )

        def start_swap(t, carry):
            swap(jnp.where(lax.rem(t, 2) == 0, chips - 1 - t // 2, t // 2)).start()
            return carry

        lax.fori_loop(0, chips, start_swap, 0)

        def add_mate(s):
            swap(s).wait_recv()
            at = at_piece(pair, s, 0)
            at[...] = at[...] + at_piece(work, s, mine)[...]

        def hop(buf, way, s, to):
            return remote(
                at_piece(buf, s, 0),
                at_piece(buf, s, 0),
                line_send.at[which, way, s],
                line_recv.at[which, way, s],
                to,
            )

        def hop_first(buf, way, s, to):
            return remote(
                at_piece(pair, s, 0),
                at_piece(buf, s, 0),
                line_send.at[which, way, s],
                line_recv.at[which, way, s],
                to,
            )

        def add_own(buf, s):
            at = at_piece(buf, s, 0)
            at[...] = at[...] + at_piece(pair, s, 0)[...]

        def reduce_step(k, carry):
            s = chips - 1 - k + chip

            @pl.when((k >= chip) & (chip < chips - 1))
            def _():
                add_mate(s)

                @pl.when(chip > 0)
                def _():
                    hop(to_right, 0, s, right).wait_recv()
                    add_own(to_right, s)
                    hop(to_right, 0, s, right).start()

                @pl.when(chip == 0)
                def _():
                    hop_first(to_right, 0, s, right).start()

            z = k - (chips - 1 - chip)

            @pl.when((z >= 0) & (chip > 0))
            def _():
                add_mate(z)

                @pl.when(chip < chips - 1)
                def _():
                    hop(to_left, 1, z, left).wait_recv()
                    add_own(to_left, z)
                    hop(to_left, 1, z, left).start()

                @pl.when(chip == chips - 1)
                def _():
                    hop_first(to_left, 1, z, left).start()

            return carry

        reduce_step(0, 0)
        meanwhile()
        lax.fori_loop(1, chips - 1, reduce_step, 0)
        add_mate(chip)

        mine_here = at_piece(pair, chip, 0)

        @pl.when(chip > 0)
        def _():
            hop(to_right, 0, chip, right).wait_recv()
            mine_here[...] = mine_here[...] + at_piece(to_right, chip, 0)[...]

        @pl.when(chip < chips - 1)
        def _():
            hop(to_left, 1, chip, left).wait_recv()
            mine_here[...] = mine_here[...] + at_piece(to_left, chip, 0)[...]

        at_piece(full, chip, mine)[...] = mine_here[...] * (1.0 / n_dp)

        def spread(way, s, to):
            return remote(
                at_piece(full, s, mine),
                at_piece(full, s, mine),
                line_send.at[which, 2 + way, s],
                line_recv.at[which, 2 + way, s],
                to,
            )

        def to_mate(s):
            return remote(
                at_piece(full, s, mine),
                at_piece(full, s, mine),
                mate_send.at[which, s],
                mate_recv.at[which, s],
                mate,
            )

        def from_mate(s):
            return remote(
                at_piece(full, s, theirs),
                at_piece(full, s, theirs),
                mate_send.at[which, s],
                mate_recv.at[which, s],
                mate,
            )

        def spread_step(t, carry):
            s = chip - t

            @pl.when(s >= 0)
            def _():
                @pl.when(t > 0)
                def _():
                    spread(0, s, right).wait_recv()

                @pl.when(chip < chips - 1)
                def _():
                    spread(0, s, right).start()

            z = chip + t

            @pl.when(z < chips)
            def _():
                @pl.when(t > 0)
                def _():
                    spread(1, z, left).wait_recv()

                @pl.when(chip > 0)
                def _():
                    spread(1, z, left).start()

            @pl.when(s >= 0)
            def _():
                to_mate(s).start()

            @pl.when((z < chips) & (t > 0))
            def _():
                to_mate(z).start()

            return carry

        lax.fori_loop(0, chips, spread_step, 0)

        def drain(s, carry):
            from_mate(s).wait_recv()
            swap(s).wait_send()
            to_mate(s).wait_send()

            @pl.when(chip < s)
            def _():
                hop(to_right, 0, s, right).wait_send()

            @pl.when(chip > s)
            def _():
                hop(to_left, 1, s, left).wait_send()

            @pl.when((s <= chip) & (chip < chips - 1))
            def _():
                spread(0, s, right).wait_send()

            @pl.when((s >= chip) & (chip > 0))
            def _():
                spread(1, s, left).wait_send()

            return carry

        lax.fori_loop(0, chips, drain, 0)

    def send_block(buf, which):
        for j in range(1, n_mp):
            remote(
                buf, buf, block_send.at[which, j], block_recv.at[which], (dp, lax.rem(mp + j, n_mp))
            ).start()

    def wait_block(buf, which):
        @pl.when(mp == owner)
        def _():
            for j in range(1, n_mp):
                remote(
                    buf,
                    buf,
                    block_send.at[which, j],
                    block_recv.at[which],
                    (dp, lax.rem(mp + j, n_mp)),
                ).wait_send()

        @pl.when(mp != owner)
        def _():
            remote(
                buf, buf, block_send.at[which, 1], block_recv.at[which], (dp, lax.rem(mp + 1, n_mp))
            ).wait_recv()

    def pick_block(full, buf):
        shift = lax.rem(small_pad - lax.rem(dp, per_shard) * block, small_pad)
        rolled = pltpu.roll(full[:, :small_pad], shift, 1)
        buf[...] = rolled[:, : buf.shape[1]]

    for i in first_loads:
        loads[i].wait()
    pay_a[...] = jnp.zeros_like(pay_a)
    pay_a[0, :, : tokens + rank] = fold3(project(q_up, 0, up_grad, eur, False))
    pay_a[1, :, : tokens + rank] = fold3(project(q_down, 0, out_grad, edr, False))
    total = sum_over_mp(pay_a, got_a, 0)

    for work in (work_p, work_q):
        for a, b in ((small // LANES * LANES, small_pad), (small_pad + large, work.shape[1])):
            if b > a:
                work[:, a:b] = jnp.zeros((rank, b - a), F32)
    for i in second_loads:
        loads[i].wait()
    expand(total[0, :, : tokens + rank], layer_in, eul, work_p, 0)
    expand(total[1, :, : tokens + rank], hidden, edl, work_p, small_pad)
    all_reduce(work_p, pair_p, right_p, left_p, full_p, 0, lambda: None)

    @pl.when(mp == owner)
    def _():
        pick_block(full_p, p_block)
        send_block(p_block, 0)

    for i, (start, rows, err) in enumerate(((0, layer_in, eul), (small_pad, hidden, edl))):
        first, second = gram_and_projections(project(full_p, start, rows, err, True), tokens)
        pay_b[i, :, :tokens] = first
        pay_b[i, :, tokens:] = second
    total = sum_over_mp(pay_b, got_b, 1)
    inv_up, inv_down = inverse_factors(total[0, :, tokens:], total[1, :, tokens:])
    t_up = dot_small(inv_up, total[0])[:, : tokens + rank]
    t_down = dot_small(inv_down, total[1])[:, : tokens + rank]
    expand(t_down, out_grad, edr, work_q, 0)
    expand(t_up, up_grad, eur, work_q, small_pad)

    def orthonormal():
        step = chunk_of(large)

        def body(i, carry):
            at = pl.multiple_of(i * step, LANES)
            orth = dot_small(inv_down, full_p[:, pl.ds(small_pad + at, step)])
            b_down[:, pl.ds(at, step)] = split_right(orth)
            return carry

        lax.fori_loop(0, large // step, body, 0, unroll=True)

    all_reduce(work_q, pair_q, right_q, left_q, full_q, 1, orthonormal)

    @pl.when(mp == owner)
    def _():
        pick_block(full_q, q_block)
        send_block(q_block, 1)

    wait_block(p_block, 0)
    a_up[...] = dot_small(inv_up, p_block[...])
    for i in last_loads:
        loads[i].wait()
    wait_block(q_block, 1)


def split_right(x):
    hi = x.astype(BF16)
    return jnp.concatenate([hi, (x - hi.astype(F32)).astype(BF16), hi], axis=0)


def split_left(x):
    hi = x.astype(BF16).astype(F32)
    return jnp.concatenate([hi, hi, x - hi], axis=0).T.astype(BF16)


def momentum_kernel(
    small,
    full_q,
    m_up,
    m_down,
    b_down,
    a_up,
    a_down,
    q_up_out,
    q_down_out,
    out_up,
    out_down,
    buf_up,
    buf_down,
    left_up,
    left_down,
    q_small,
    sem_up,
    sem_down,
    sem_q,
):
    block, large = m_up.shape
    step = buf_up.shape[2]
    start = whole_tiles(small)
    q_small[...] = full_q[:, :small]
    q_copies = (
        pltpu.make_async_copy(full_q.at[:, pl.ds(start, large)], q_up_out, sem_q.at[0]),
        pltpu.make_async_copy(q_small, q_down_out, sem_q.at[1]),
    )
    left_up[...] = split_left(a_up[...])[:block]
    left_down[...] = split_left(a_down[...])[:block]

    def copy(buf, out, sem, i):
        columns = pl.ds(pl.multiple_of(i * step, LANES), step)
        return pltpu.make_async_copy(buf.at[i % 2], out.at[:, columns], sem.at[i % 2])

    def body(i, carry):
        at = pl.multiple_of(i * step, LANES)
        columns = pl.ds(at, step)
        q = split_right(full_q[:, pl.ds(start + at, step)])
        for m, a, b, buf, out, sem in (
            (m_up, left_up, q, buf_up, out_up, sem_up),
            (m_down, left_down, b_down[:, columns], buf_down, out_down, sem_down),
        ):

            @pl.when(i >= 2)
            def _():
                copy(buf, out, sem, i - 2).wait()

            delta = dot_nn(a[...], b)
            buf[i % 2] = (0.9 * m[:, columns].astype(F32) + delta).astype(BF16)
            copy(buf, out, sem, i).start()
        return carry

    count = large // step
    lax.fori_loop(0, count, body, 0)
    for c in q_copies:
        c.start()
    for i in range(max(count - 2, 0), count):
        copy(buf_up, out_up, sem_up, i).wait()
        copy(buf_down, out_down, sem_down, i).wait()
    for c in q_copies:
        c.wait()


def on_device(
    layer_in,
    up_grad,
    hidden,
    out_grad,
    err_up_left,
    err_up_right,
    err_down_left,
    err_down_right,
    q_up,
    q_down,
    momentum_up,
    momentum_down,
):
    n_dp = lax.axis_size("dp")
    n_mp = lax.axis_size("mp")
    chips = n_dp // 2
    tokens, small = layer_in.shape
    large = hidden.shape[1]
    rank = q_up.shape[1]
    block = momentum_up.shape[0]
    block_pad = whole_tiles(block)
    pieces = n_dp // 4
    piece = -(-((whole_tiles(small) + large) // LANES) // pieces) * LANES
    half = piece * pieces // 2
    vmem = pl.BlockSpec(memory_space=pltpu.VMEM)
    hbm = pl.BlockSpec(memory_space=pltpu.HBM)
    dma = pltpu.SemaphoreType.DMA
    operands = (
        layer_in,
        up_grad,
        hidden,
        out_grad,
        err_up_left[0].T,
        err_up_right[0].T,
        err_down_left[0].T,
        err_down_right[0].T,
        q_up.T,
        q_down.T,
        momentum_up,
        momentum_down.T,
    )
    operands = tuple(pltpu.with_memory_space_constraint(x, pltpu.HBM) for x in operands)
    whole = pltpu.VMEM((rank, 2 * half), F32)
    part = pltpu.VMEM((rank, half), F32)
    pay = pltpu.VMEM((2, rank, tokens + 4 * rank), F32)
    got = pltpu.VMEM((n_mp, 2, rank, tokens + 4 * rank), F32)
    full_q, m_up, m_down, b_down, a_up, a_down = pl.pallas_call(
        functools.partial(exchange_kernel, n_dp, n_mp),
        out_shape=(
            jax.ShapeDtypeStruct((rank, 2 * half), F32),
            jax.ShapeDtypeStruct((block, large), BF16),
            jax.ShapeDtypeStruct((block, large), BF16),
            jax.ShapeDtypeStruct((3 * rank, large), BF16),
            jax.ShapeDtypeStruct((rank, block_pad), F32),
            jax.ShapeDtypeStruct((rank, block_pad), F32),
        ),
        in_specs=[hbm] * 12,
        out_specs=[vmem] * 6,
        scratch_shapes=[
            *[pltpu.VMEM(x.shape, x.dtype) for x in operands[:10]],
            pay,
            got,
            pay,
            got,
            *[whole, part, part, part, whole],
            *[whole, part, part, part],
            pltpu.VMEM((rank, block_pad), F32),
            dma((12,)),
            dma((2, n_mp)),
            dma((2, n_mp)),
            dma((2, chips)),
            dma((2, chips)),
            dma((2, 4, chips)),
            dma((2, 4, chips)),
            dma((2, chips)),
            dma((2, chips)),
            dma((2, n_mp)),
            dma((2,)),
        ],
        compiler_params=pltpu.CompilerParams(
            collective_id=0, has_side_effects=True, vmem_limit_bytes=26 * 1024 * 1024
        ),
    )(*operands)
    step = chunk_of(large)
    slots = pltpu.VMEM((2, block, step), BF16)
    left = pltpu.VMEM((block, 3 * rank), BF16)
    q_up_t, q_down_t, new_up, new_down_t = pl.pallas_call(
        functools.partial(momentum_kernel, small),
        out_shape=(
            jax.ShapeDtypeStruct((rank, large), F32),
            jax.ShapeDtypeStruct((rank, small), F32),
            jax.ShapeDtypeStruct((block, large), BF16),
            jax.ShapeDtypeStruct((block, large), BF16),
        ),
        in_specs=[vmem] * 6,
        out_specs=[hbm] * 4,
        scratch_shapes=[
            slots,
            slots,
            left,
            left,
            pltpu.VMEM((rank, small), F32),
            dma((2,)),
            dma((2,)),
            dma((2,)),
        ],
        compiler_params=pltpu.CompilerParams(vmem_limit_bytes=16 * 1024 * 1024),
    )(full_q, m_up, m_down, b_down, a_up, a_down)
    return (q_up_t.T, q_down_t.T, new_up, new_down_t.T)


def solution(mesh):
    return jax.shard_map(
        on_device,
        mesh=mesh,
        in_specs=(
            P("dp", "mp"),
            P("dp", "mp"),
            P("dp", "mp"),
            P("dp", "mp"),
            P("dp", "mp", None),
            P("dp", "mp", None),
            P("dp", "mp", None),
            P("dp", "mp", None),
            P("mp", None),
            P("mp", None),
            P("dp", "mp"),
            P("mp", "dp"),
        ),
        out_specs=(P("mp", None), P("mp", None), P("dp", "mp"), P("mp", "dp")),
        check_vma=False,
    )
```
